32 devices in a mesh: pairs: 8 (over z, x), own: 4 (over y, core).
Axes of the slice: x: 2, y: 2, z: 4, core: 2. Of those that a mesh axis runs over, the one named last changes fastest.
Arguments:
- amplitudes: bfloat16 [512, 4, 4096], P(('pairs', 'own')), may hold values from -6 to 6
- integrals: bfloat16 [4, 4096, 4, 4096], P('own', None, None, 'pairs'), may hold values from -0.046875 to 0.046875
- owner: int32 [4], replicated, may hold values from 0 to 3, each once
- amp_mask: int32 [512, 4], P(('pairs', 'own')), may hold values 0 or 1
- int_mask: int32 [4, 4], replicated, may hold values from 0 to 1, as said below
- out_mask: int32 [4], replicated, may hold values from 0 to 1, as said below
Outputs:
- ladder: bfloat16 [512, 4, 4096], P(('pairs', 'own'))
The draws below stay inside these ranges and needn't reach their ends.
Inputs may be any that keep to these rules, and one draw needn't show every extreme that they name: `int_mask`: every column has a 1 in some row. `out_mask`: at least one entry is 1. `owner`: each slot holds exactly one piece.
All inputs are finite; a program needn't handle non-finite values. No bound on the sum of `amp_mask` on one device may be relied on, other than what follows from the above.
Results may differ from the reference program's by a relative error of at most 0.001.
Values may be sent and summed in bfloat16 or wider, within the bound.
A program may use at most 128 MiB of HBM per device.

```python
import jax
import jax.numpy as jnp
from jax import lax

TP = 4096
NCD = 4
NAB = 4
ROWS = 512
PIECE = 4096
N_OWN = 4


def draw_int_mask(key, part):
    random_bits = jax.random.randint(jax.random.fold_in(key, 11), (NCD, NAB), 0, 2)
    chosen = jax.random.randint(jax.random.fold_in(key, 13), (NAB,), 0, NCD)
    forced = (jnp.arange(NCD)[:, None] == chosen[None, :]).astype(jnp.int32)
    return jnp.maximum(random_bits, forced).astype(jnp.int32)


def draw_out_mask(key, part):
    random_bits = jax.random.randint(jax.random.fold_in(key, 17), (NAB,), 0, 2)
    chosen = jax.random.randint(jax.random.fold_in(key, 19), (), 0, NAB)
    forced = (jnp.arange(NAB) == chosen).astype(jnp.int32)
    return jnp.maximum(random_bits, forced).astype(jnp.int32)


def touch_ends(array, key, smallest, high):
    longest = array.shape.index(max(array.shape))
    spots = []
    for shift in (0, 1):
        where = [jax.random.randint(jax.random.fold_in(key, axis), (), 0, length) for axis, length in enumerate(array.shape)]
        where[longest] = (where[longest] + shift) % array.shape[longest]
        spots.append(tuple(where))
    return array.at[spots[0]].set(smallest).at[spots[1]].set(high)


def steps_of(stream_key, shape, cuts, least, high):
    def one(dim, shards_of):
        steps = jax.random.uniform(jax.random.fold_in(jax.random.fold_in(stream_key, 6), dim), (shards_of,), jnp.float32, least / len(cuts), high / len(cuts))
        return jnp.repeat(jnp.exp(steps), shape[dim] // shards_of).reshape((-1,) + (1,) * (len(shape) - dim - 1))

    loudness = one(*cuts[0])
    for cut in cuts[1:]:
        loudness = loudness * one(*cut)
    return loudness


def centred(key, shape, spread, limit, split=(), kind=jnp.bfloat16):
    values = spread * jax.random.normal(key, shape, jnp.float32)
    if split:
        values = values * steps_of(key, shape, split, -0.22, 0.18)
    return jnp.clip(values, -limit, limit).astype(kind)


def setup_inputs(seed: int = 0) -> dict:
    key_of = jax.random.split(jax.random.key(seed), 7)
    amplitudes = centred(key_of[0], (ROWS, NCD, TP), 1.0, 6.0, ((0, 32),))
    integrals = centred(key_of[1], (N_OWN, PIECE, NAB, TP), (NCD * TP) ** -0.5, 0.046875, ((0, 4), (3, 8)))
    owner = jax.random.permutation(key_of[2], N_OWN).astype(jnp.int32)
    amp_mask = touch_ends((jax.random.randint(key_of[3], (ROWS, NCD), 0, 4) < 3).astype(jnp.int32), jax.random.fold_in(key_of[3], 1), 0, 1)
    int_mask = draw_int_mask(jax.random.fold_in(key_of[6], 71), 0)
    out_mask = draw_out_mask(jax.random.fold_in(key_of[6], 71), 0)
    return dict(amplitudes=amplitudes, integrals=integrals, owner=owner, amp_mask=amp_mask, int_mask=int_mask, out_mask=out_mask)


def reference(amplitudes, integrals, owner, amp_mask, int_mask, out_mask):
    row_total = amplitudes.shape[0]
    contraction = NCD * TP
    pieces = jnp.take(integrals, owner.astype(jnp.int32), axis=0).reshape(contraction, NAB, TP)
    panel_ids = jnp.arange(contraction, dtype=jnp.int32) // TP
    mask_table = int_mask.astype(jnp.float32)
    factor = jnp.take(mask_table, panel_ids, axis=0).astype(pieces.dtype)
    masked_v = pieces * factor[:, :, None]
    masked_t = amplitudes * amp_mask.astype(amplitudes.dtype)[:, :, None]
    amp_flat = masked_t.reshape(row_total, contraction)

    def one_tile(tile_index):
        tile_slab = lax.dynamic_index_in_dim(masked_v, tile_index, 1, keepdims=False)
        return jnp.dot(amp_flat, tile_slab, preferred_element_type=jnp.float32)

    summed = lax.map(one_tile, jnp.arange(NAB, dtype=jnp.int32))
    weighted = jnp.transpose(summed, (1, 0, 2)) * out_mask.astype(jnp.float32)[None, :, None]
    return weighted.astype(jnp.bfloat16)
```

```python
import jax
import jax.numpy as jnp
from jax import lax
from jax.sharding import PartitionSpec as P


def local(amplitudes, integrals, owner, amp_mask, int_mask, out_mask):
    own_count = lax.axis_size("own")
    pairs_count = lax.axis_size("pairs")
    slab = integrals[0]
    piece_rows, tile_count, col_count = slab.shape
    pair_rows, panel_count, tile_pair = amplitudes.shape
    rows = pair_rows * pairs_count * own_count
    slots = jnp.arange(own_count, dtype=jnp.int32)
    piece_of = jnp.sum(jnp.where(owner[:, None] == slots[None, :], slots[:, None], 0), axis=0)
    my_piece = piece_of[lax.axis_index("own")]
    my_tile = my_piece * piece_rows // tile_pair
    masked_t = amplitudes * amp_mask.astype(amplitudes.dtype)[:, :, None]
    pieces = masked_t.reshape(pair_rows, own_count, piece_rows)
    ordered = jnp.stack(
        [lax.dynamic_index_in_dim(pieces, piece_of[slot], 1, keepdims=False) for slot in range(own_count)], axis=1
    )
    mine = lax.all_to_all(ordered, "own", split_axis=1, concat_axis=0, tiled=True)
    gathered = lax.all_gather(mine.reshape(own_count * pair_rows, piece_rows), "pairs", axis=0, tiled=True)
    summed = jnp.dot(gathered, slab.reshape(piece_rows, tile_count * col_count), preferred_element_type=jnp.float32)
    keep = (int_mask[my_tile] * out_mask).astype(jnp.float32)
    part = summed.reshape(pairs_count, own_count, pair_rows, tile_count, col_count) * keep[:, None]
    total = lax.psum_scatter(part, "own", scatter_dimension=1, tiled=False)
    rounded = total.astype(jnp.bfloat16)
    moved = lax.all_to_all(rounded, "pairs", split_axis=0, concat_axis=3, tiled=True)
    return moved[0]


def solution(mesh):
    return jax.shard_map(
        local,
        mesh=mesh,
        in_specs=(
            P(("pairs", "own"), None, None),
            P("own", None, None, "pairs"),
            P(),
            P(("pairs", "own"), None),
            P(),
            P(),
        ),
        out_specs=P(("pairs", "own"), None, None),
        check_vma=False,
    )
```

```python
import functools
import math

import jax
import jax.numpy as jnp
from jax import lax
from jax.experimental import pallas as pl
from jax.experimental.pallas import tpu as pltpu
from jax.sharding import PartitionSpec as P

MESH = pl.DeviceIdType.MESH
CHUNK = 256


def kernel(sizes, t_ref, v_ref, keep_ref, out_ref, tbuf, vbuf, stage, part, core_in, side_in, done,
           v_sem, own_send, own_recv, z_send, z_recv, x_send, x_recv, c_send, c_recv, y_send, y_recv, o_send, o_recv):
    Z, X, Y, K, N, cols, step_cols = sizes
    O, PAIRS = 2 * Y, Z * X
    pair, own = lax.axis_index("pairs"), lax.axis_index("own")
    z, x = pair // X, pair % X
    y, c = own // 2, own % 2

    def own_at(fy, fc):
        return ((y + Y + fy) % Y) * 2 + (c + 2 + fc) % 2

    def pair_at(d, e):
        return ((z + Z + d) % Z) * X + (x + X + e) % X

    def remote(src, dst, send, recv, device):
        return pltpu.make_async_remote_copy(
            src_ref=src, dst_ref=dst, send_sem=send, recv_sem=recv, device_id=device, device_id_type=MESH
        )

    barrier = pltpu.get_barrier_semaphore()
    for f in range(1, O):
        pl.semaphore_signal(barrier, inc=1, device_id={"own": (own + f) % O}, device_id_type=MESH)
    for g in range(1, PAIRS):
        pl.semaphore_signal(barrier, inc=1, device_id={"pairs": (pair + g) % PAIRS}, device_id_type=MESH)

    chunks = K // CHUNK

    def load(i, slot):
        rows = pl.ds(pl.multiple_of(i * CHUNK, CHUNK), CHUNK)
        return pltpu.make_async_copy(v_ref.at[rows], stage.at[slot], v_sem.at[slot])

    load(0, 0).start()
    load(1, 1).start()
    pl.semaphore_wait(barrier, O - 1 + PAIRS - 1)

    own_copies = []
    for f in range(1, O):
        fy, fc = f // 2, f % 2
        to = own_at(fy, fc)
        copy = remote(t_ref.at[to], tbuf.at[0, 0, fc, fy], own_send.at[f], own_recv.at[f], {"own": to})
        copy.start()
        own_copies.append(copy)
    tbuf[0, 0, 0, 0] = t_ref[own]
    for copy in own_copies:
        copy.wait_recv()

    z_copies = {}
    for d in range(1, Z):
        z_copies[d] = remote(tbuf.at[0, 0], tbuf.at[d, 0], z_send.at[d], z_recv.at[d], {"pairs": pair_at(d, 0)})
        z_copies[d].start()
    x_copies = {}

    def forward(d):
        for e in range(1, X):
            x_copies[d, e] = remote(
                tbuf.at[d, 0], tbuf.at[d, e], x_send.at[d, e], x_recv.at[d, e], {"pairs": pair_at(0, e)}
            )
            x_copies[d, e].start()

    forward(0)

    def flatten(first, last):
        @pl.loop(first // 2, last // 2)
        def _(pairno):
            for slot in range(2):
                i = pairno * 2 + slot
                load(i, slot).wait()
                rows = pl.ds(pl.multiple_of(i * CHUNK, CHUNK), CHUNK)
                vbuf[rows, :] = stage[slot].reshape(CHUNK, N)

                @pl.when(i + 2 < chunks)
                def _():
                    load(i + 2, slot).start()

    flatten(0, chunks)

    c_copies, y_copies, o_copies = {}, {}, []

    def multiply(d):
        rows = tbuf.at[d]

        @pl.loop(0, N // step_cols)
        def _(n):
            at = pl.ds(pl.multiple_of(n * step_cols, step_cols), step_cols)
            a = rows[...].reshape(X * O * 16, K)
            product = jnp.dot(a, vbuf[:, at], preferred_element_type=jnp.float32)
            scale = keep_ref[n * step_cols // cols]
            part[d, :, :, :, :, at] = (product * scale).reshape(X, 2, Y, 16, step_cols)

        c_copies[d] = remote(part.at[d, :, 1], core_in.at[d], c_send.at[d], c_recv.at[d], {"own": own_at(0, 1)})
        c_copies[d].start()

    def add_core(d):
        c_copies[d].wait_recv()
        for e in range(X):
            for fy in range(Y):
                part[d, e, 0, fy] = part[d, e, 0, fy] + core_in[d, e, fy]
        for fy in range(1, Y):
            y_copies[d, fy] = remote(
                part.at[d, :, 0, fy], side_in.at[d, fy], y_send.at[d, fy], y_recv.at[d, fy], {"own": own_at(-fy, 0)}
            )
            y_copies[d, fy].start()

    def add_side(d):
        for fy in range(1, Y):
            y_copies[d, fy].wait_recv()
        for e in range(X):
            total = part[d, e, 0, 0]
            for fy in range(1, Y):
                total = total + side_in[d, fy, e]
            rounded = total.astype(jnp.bfloat16)
            if d == 0 and e == 0:
                out_ref[pair] = rounded
            else:
                done[d, e] = rounded
                copy = remote(done.at[d, e], out_ref.at[pair], o_send.at[d, e], o_recv.at[d, e], {"pairs": pair_at(-d, -e)})
                copy.start()
                o_copies.append(copy)

    for d in range(Z):
        if d + 1 < Z:
            z_copies[d + 1].wait_recv()
            forward(d + 1)
        for e in range(1, X):
            x_copies[d, e].wait_recv()
        multiply(d)
        if d >= 1:
            add_core(d - 1)
        if d >= 2:
            add_side(d - 2)
    add_core(Z - 1)
    if Z >= 2:
        add_side(Z - 2)
    add_side(Z - 1)
    for copy in o_copies:
        copy.wait_recv()
    for group in (own_copies, z_copies.values(), x_copies.values(), c_copies.values(), y_copies.values(), o_copies):
        for copy in group:
            copy.wait_send()


def local(amplitudes, integrals, owner, amp_mask, int_mask, out_mask):
    own_count = lax.axis_size("own")
    pairs_count = lax.axis_size("pairs")
    slab = integrals[0]
    piece_rows, tile_count, col_count = slab.shape
    pair_rows, panel_count, tile_pair = amplitudes.shape
    width = tile_count * col_count
    X = math.isqrt(pairs_count // 2)
    Z = pairs_count // X
    Y = own_count // 2
    slots = jnp.arange(own_count, dtype=jnp.int32)
    piece_of = jnp.sum(jnp.where(owner[:, None] == slots[None, :], slots[:, None], 0), axis=0)
    my_piece = piece_of[lax.axis_index("own")]
    my_tile = my_piece * piece_rows // tile_pair
    keep = (int_mask[my_tile] * out_mask).astype(jnp.float32)
    masked_t = amplitudes * amp_mask.astype(amplitudes.dtype)[:, :, None]
    pieces = masked_t.reshape(pair_rows, own_count, piece_rows)
    ordered = jnp.stack(
        [lax.dynamic_index_in_dim(pieces, piece_of[slot], 1, keepdims=False) for slot in range(own_count)], axis=0
    )
    step_cols = min(256, col_count)
    sizes = (Z, X, Y, piece_rows, width, col_count, step_cols)
    dma = lambda *shape: pltpu.SemaphoreType.DMA(shape)
    vmem = pl.BlockSpec(memory_space=pltpu.VMEM)
    moved = pl.pallas_call(
        functools.partial(kernel, sizes),
        out_shape=jax.ShapeDtypeStruct((pairs_count, pair_rows, width), jnp.bfloat16),
        in_specs=[vmem, pl.BlockSpec(memory_space=pl.ANY), pl.BlockSpec(memory_space=pltpu.SMEM)],
        out_specs=vmem,
        scratch_shapes=[
            pltpu.VMEM((Z, X, 2, Y, pair_rows, piece_rows), jnp.bfloat16),
            pltpu.VMEM((piece_rows, width), jnp.bfloat16),
            pltpu.VMEM((2, CHUNK, tile_count, col_count), jnp.bfloat16),
            pltpu.VMEM((Z, X, 2, Y, pair_rows, width), jnp.float32),
            pltpu.VMEM((Z, X, Y, pair_rows, width), jnp.float32),
            pltpu.VMEM((Z, Y, X, pair_rows, width), jnp.float32),
            pltpu.VMEM((Z, X, pair_rows, width), jnp.bfloat16),
            dma(2), dma(own_count), dma(own_count), dma(Z), dma(Z), dma(Z, X), dma(Z, X),
            dma(Z), dma(Z), dma(Z, Y), dma(Z, Y), dma(Z, X), dma(Z, X),
        ],
        compiler_params=pltpu.CompilerParams(
            collective_id=0, has_side_effects=True, vmem_limit_bytes=60 * 1024 * 1024
        ),
        cost_estimate=pl.CostEstimate(
            flops=2 * pairs_count * own_count * pair_rows * piece_rows * width,
            bytes_accessed=2 * piece_rows * width, transcendentals=0,
        ),
    )(ordered, slab, keep)
    shaped = moved.reshape(pairs_count, pair_rows, tile_count, col_count)
    return jnp.transpose(shaped, (1, 2, 0, 3)).reshape(pair_rows, tile_count, pairs_count * col_count)


def solution(mesh):
    return jax.shard_map(
        local,
        mesh=mesh,
        in_specs=(
            P(("pairs", "own"), None, None),
            P("own", None, None, "pairs"),
            P(),
            P(("pairs", "own"), None),
            P(),
            P(),
        ),
        out_specs=P(("pairs", "own"), None, None),
        check_vma=False,
    )
```

```python
import functools
import math

import jax
import jax.numpy as jnp
from jax import lax
from jax.experimental import pallas as pl
from jax.experimental.pallas import tpu as pltpu
from jax.sharding import PartitionSpec as P

MESH = pl.DeviceIdType.MESH
CHUNK = 256


def kernel(sizes, t_ref, v_ref, keep_ref, out_ref, tbuf, vbuf, stage, part, core_in, side_in, done,
           v_sem, own_send, own_recv, z_send, z_recv, x_send, x_recv, c_send, c_recv, y_send, y_recv, o_send, o_recv):
    Z, X, Y, K, N, cols, step_cols = sizes
    O, PAIRS = 2 * Y, Z * X
    pair, own = lax.axis_index("pairs"), lax.axis_index("own")
    z, x = pair // X, pair % X
    y, c = own // 2, own % 2
    near = jnp.minimum(z, Z - 1 - z)
    longer = jnp.where(2 * z < Z - 1, 1, -1)

    def own_at(fy, fc):
        return ((y + Y + fy) % Y) * 2 + (c + 2 + fc) % 2

    def x_at(e):
        return (x + X + e) % X

    def source(t):
        if t == 0:
            return z
        both = z + (t + 1) // 2 * (1 if t % 2 else -1)
        return jnp.where(t <= 2 * near, both, z + longer * (t - near))

    def remote(src, dst, send, recv, device):
        return pltpu.make_async_remote_copy(
            src_ref=src, dst_ref=dst, send_sem=send, recv_sem=recv, device_id=device, device_id_type=MESH
        )

    barrier = pltpu.get_barrier_semaphore()
    for f in range(1, O):
        pl.semaphore_signal(barrier, inc=1, device_id={"own": (own + f) % O}, device_id_type=MESH)
    for g in range(1, PAIRS):
        pl.semaphore_signal(barrier, inc=1, device_id={"pairs": (pair + g) % PAIRS}, device_id_type=MESH)

    chunks = K // CHUNK

    def load(i, slot):
        rows = pl.ds(pl.multiple_of(i * CHUNK, CHUNK), CHUNK)
        return pltpu.make_async_copy(v_ref.at[rows], stage.at[slot], v_sem.at[slot])

    load(0, 0).start()
    load(1, 1).start()
    pl.semaphore_wait(barrier, O - 1 + PAIRS - 1)

    own_copies = {}
    for f in range(1, O):
        fy, fc = f // 2, f % 2
        to = own_at(fy, fc)
        own_copies[f] = remote(t_ref.at[to], tbuf.at[z, 0, fy, fc], own_send.at[f], own_recv.at[f], {"own": to})
        own_copies[f].start()
    tbuf[z, 0, 0, 0] = t_ref[own]

    def z_copy(t, h, up):
        s = source(t)
        to = jnp.where(up == 1, jnp.minimum(z + 1, Z - 1), jnp.maximum(z - 1, 0))
        block = tbuf.at[s, 0, h]
        return remote(block, block, z_send.at[t, h, up], z_recv.at[s, h], {"pairs": to * X + x})

    def z_needed(t, up):
        s = source(t)
        if up:
            return jnp.logical_and(s <= z, z + 1 < Z)
        return jnp.logical_and(s >= z, z >= 1)

    def x_copy(t, h, e):
        s = source(t)
        return remote(
            tbuf.at[s, 0, h], tbuf.at[s, e, h], x_send.at[t, h, e], x_recv.at[t, h, e], {"pairs": z * X + x_at(e)}
        )

    def arrive(t, h):
        if t == 0:
            for fc in range(2):
                if 2 * h + fc:
                    own_copies[2 * h + fc].wait_recv()
        else:
            z_copy(t, h, 0).wait_recv()
        for up in range(2):
            @pl.when(z_needed(t, up))
            def _():
                z_copy(t, h, up).start()
        for e in range(1, X):
            x_copy(t, h, e).start()

    def flatten(first, last):
        @pl.loop(first // 2, last // 2)
        def _(pairno):
            for slot in range(2):
                i = pairno * 2 + slot
                load(i, slot).wait()
                rows = pl.ds(pl.multiple_of(i * CHUNK, CHUNK), CHUNK)
                vbuf[rows, :] = stage[slot].reshape(CHUNK, N)

                @pl.when(i + 2 < chunks)
                def _():
                    load(i + 2, slot).start()

    c_copies, y_copies = {}, {}

    def multiply(t):
        s = source(t)
        for e in range(1, X):
            for h in range(Y):
                x_copy(t, h, e).wait_recv()

        @pl.loop(0, N // step_cols)
        def _(n):
            at = pl.ds(pl.multiple_of(n * step_cols, step_cols), step_cols)
            rows = tbuf[s].reshape(X * O * 16, K)
            product = jnp.dot(rows, vbuf[:, at], preferred_element_type=jnp.float32)
            scale = keep_ref[n * step_cols // cols]
            part[t, :, :, :, :, at] = (product * scale).reshape(X, Y, 2, 16, step_cols)

        c_copies[t] = remote(part.at[t, :, :, 1], core_in.at[t], c_send.at[t], c_recv.at[t], {"own": own_at(0, 1)})
        c_copies[t].start()

    def add_core(t):
        c_copies[t].wait_recv()
        for fy in list(range(1, Y)) + [0]:
            for e in range(X):
                part[t, e, fy, 0] = part[t, e, fy, 0] + core_in[t, e, fy]
            if fy:
                y_copies[t, fy] = remote(
                    part.at[t, :, fy, 0], side_in.at[t, fy], y_send.at[t, fy], y_recv.at[t, fy],
                    {"own": own_at(-fy, 0)},
                )
                y_copies[t, fy].start()

    def o_copy(t, e):
        return remote(
            done.at[t, e], out_ref.at[pair], o_send.at[t, e], o_recv.at[z, e], {"pairs": source(t) * X + x_at(-e)}
        )

    def add_side(t):
        for fy in range(1, Y):
            y_copies[t, fy].wait_recv()
        for e in range(X):
            total = part[t, e, 0, 0]
            for fy in range(1, Y):
                total = total + side_in[t, fy, e]
            rounded = total.astype(jnp.bfloat16)
            if t == 0 and e == 0:
                out_ref[pair] = rounded
            else:
                done[t, e] = rounded
                o_copy(t, e).start()

    early = [(0, h) for h in range(Y)] + [(t, h) for h in range(Y) for t in range(1, min(3, Z))]
    cuts = [chunks * k // (len(early) - 1) // 2 * 2 for k in range(len(early))]
    for k, (t, h) in enumerate(early):
        if k:
            flatten(cuts[k - 1], cuts[k])
        arrive(t, h)
    for t in range(Z):
        if t >= 1 and t + 2 < Z:
            for h in range(Y):
                arrive(t + 2, h)
        multiply(t)
        if t >= 1:
            add_core(t - 1)
        if t >= 2:
            add_side(t - 2)
    add_core(Z - 1)
    add_side(Z - 2)
    add_side(Z - 1)
    for t in range(Z):
        for e in range(X):
            if t or e:
                s = source(t)
                remote(
                    done.at[t, e], out_ref.at[s * X + x_at(e)], o_send.at[t, e], o_recv.at[s, e], {"pairs": s * X + x_at(e)}
                ).wait_recv()
                o_copy(t, e).wait_send()
    for t in range(Z):
        for h in range(Y):
            for up in range(2):
                @pl.when(z_needed(t, up))
                def _():
                    z_copy(t, h, up).wait_send()
            for e in range(1, X):
                x_copy(t, h, e).wait_send()
    for group in (own_copies, c_copies, y_copies):
        for copy in group.values():
            copy.wait_send()


def local(amplitudes, integrals, owner, amp_mask, int_mask, out_mask):
    own_count = lax.axis_size("own")
    pairs_count = lax.axis_size("pairs")
    slab = integrals[0]
    piece_rows, tile_count, col_count = slab.shape
    pair_rows, panel_count, tile_pair = amplitudes.shape
    width = tile_count * col_count
    X = math.isqrt(pairs_count // 2)
    Z = pairs_count // X
    Y = own_count // 2
    slots = jnp.arange(own_count, dtype=jnp.int32)
    piece_of = jnp.sum(jnp.where(owner[:, None] == slots[None, :], slots[:, None], 0), axis=0)
    my_piece = piece_of[lax.axis_index("own")]
    my_tile = my_piece * piece_rows // tile_pair
    keep = (int_mask[my_tile] * out_mask).astype(jnp.float32)
    masked_t = amplitudes * amp_mask.astype(amplitudes.dtype)[:, :, None]
    pieces = masked_t.reshape(pair_rows, own_count, piece_rows)
    ordered = jnp.stack(
        [lax.dynamic_index_in_dim(pieces, piece_of[slot], 1, keepdims=False) for slot in range(own_count)], axis=0
    )
    step_cols = min(256, col_count)
    sizes = (Z, X, Y, piece_rows, width, col_count, step_cols)
    dma = lambda *shape: pltpu.SemaphoreType.DMA(shape)
    vmem = pl.BlockSpec(memory_space=pltpu.VMEM)
    moved = pl.pallas_call(
        functools.partial(kernel, sizes),
        out_shape=jax.ShapeDtypeStruct((pairs_count, pair_rows, width), jnp.bfloat16),
        in_specs=[vmem, pl.BlockSpec(memory_space=pl.ANY), pl.BlockSpec(memory_space=pltpu.SMEM)],
        out_specs=vmem,
        scratch_shapes=[
            pltpu.VMEM((Z, X, Y, 2, pair_rows, piece_rows), jnp.bfloat16),
            pltpu.VMEM((piece_rows, width), jnp.bfloat16),
            pltpu.VMEM((2, CHUNK, tile_count, col_count), jnp.bfloat16),
            pltpu.VMEM((Z, X, Y, 2, pair_rows, width), jnp.float32),
            pltpu.VMEM((Z, X, Y, pair_rows, width), jnp.float32),
            pltpu.VMEM((Z, Y, X, pair_rows, width), jnp.float32),
            pltpu.VMEM((Z, X, pair_rows, width), jnp.bfloat16),
            dma(2), dma(own_count), dma(own_count), dma(Z, Y, 2), dma(Z, Y), dma(Z, Y, X), dma(Z, Y, X),
            dma(Z), dma(Z), dma(Z, Y), dma(Z, Y), dma(Z, X), dma(Z, X),
        ],
        compiler_params=pltpu.CompilerParams(
            collective_id=0, has_side_effects=True, vmem_limit_bytes=60 * 1024 * 1024
        ),
        cost_estimate=pl.CostEstimate(
            flops=2 * pairs_count * own_count * pair_rows * piece_rows * width,
            bytes_accessed=2 * piece_rows * width, transcendentals=0,
        ),
    )(ordered, slab, keep)
    shaped = moved.reshape(pairs_count, pair_rows, tile_count, col_count)
    return jnp.transpose(shaped, (1, 2, 0, 3)).reshape(pair_rows, tile_count, pairs_count * col_count)


def solution(mesh):
    return jax.shard_map(
        local,
        mesh=mesh,
        in_specs=(
            P(("pairs", "own"), None, None),
            P("own", None, None, "pairs"),
            P(),
            P(("pairs", "own"), None),
            P(),
            P(),
        ),
        out_specs=P(("pairs", "own"), None, None),
        check_vma=False,
    )
```

```python
import functools
import math

import jax
import jax.numpy as jnp
from jax import lax
from jax.experimental import pallas as pl
from jax.experimental.pallas import tpu as pltpu
from jax.sharding import PartitionSpec as P

MESH = pl.DeviceIdType.MESH
CHUNK = 256


def kernel(sizes, t_ref, v_ref, keep_ref, out_ref, tbuf, vbuf, stage, part, core_in, side_in, done,
           v_sem, own_send, own_recv, z_send, z_recv, x_send, x_recv, c_send, c_recv, y_send, y_recv, o_send, o_recv):
    Z, X, Y, K, N, cols, step_cols = sizes
    O, PAIRS = 2 * Y, Z * X
    pair, own = lax.axis_index("pairs"), lax.axis_index("own")
    z, x = pair // X, pair % X
    y, c = own // 2, own % 2
    near = jnp.minimum(z, Z - 1 - z)
    longer = jnp.where(2 * z < Z - 1, 1, -1)

    def own_at(fy, fc):
        return ((y + Y + fy) % Y) * 2 + (c + 2 + fc) % 2

    def x_at(e):
        return (x + X + e) % X

    def source(t):
        if t == 0:
            return z
        both = z + (t + 1) // 2 * (1 if t % 2 else -1)
        return jnp.where(t <= 2 * near, both, z + longer * (t - near))

    def remote(src, dst, send, recv, device):
        return pltpu.make_async_remote_copy(
            src_ref=src, dst_ref=dst, send_sem=send, recv_sem=recv, device_id=device, device_id_type=MESH
        )

    barrier = pltpu.get_barrier_semaphore()
    for f in range(1, O):
        pl.semaphore_signal(barrier, inc=1, device_id={"own": (own + f) % O}, device_id_type=MESH)
    for g in range(1, PAIRS):
        pl.semaphore_signal(barrier, inc=1, device_id={"pairs": (pair + g) % PAIRS}, device_id_type=MESH)

    chunks = K // CHUNK

    def load(i, slot):
        rows = pl.ds(pl.multiple_of(i * CHUNK, CHUNK), CHUNK)
        return pltpu.make_async_copy(v_ref.at[rows], stage.at[slot], v_sem.at[slot])

    load(0, 0).start()
    load(1, 1).start()
    pl.semaphore_wait(barrier, O - 1 + PAIRS - 1)

    own_copies = {}
    for f in range(1, O):
        fy, fc = f // 2, f % 2
        to = own_at(fy, fc)
        own_copies[f] = remote(t_ref.at[to], tbuf.at[z, 0, fy, fc], own_send.at[f], own_recv.at[f], {"own": to})
        own_copies[f].start()
    tbuf[z, 0, 0, 0] = t_ref[own]

    def z_copy(t, h, up):
        s = source(t)
        to = jnp.where(up == 1, jnp.minimum(z + 1, Z - 1), jnp.maximum(z - 1, 0))
        block = tbuf.at[s, 0, h]
        return remote(block, block, z_send.at[t, h, up], z_recv.at[s, h], {"pairs": to * X + x})

    def z_needed(t, up):
        s = source(t)
        if up:
            return jnp.logical_and(s <= z, z + 1 < Z)
        return jnp.logical_and(s >= z, z >= 1)

    def x_copy(t, h, e):
        s = source(t)
        return remote(
            tbuf.at[s, 0, h], tbuf.at[s, e, h], x_send.at[t, h, e], x_recv.at[t, h, e], {"pairs": z * X + x_at(e)}
        )

    def arrive(t, h):
        if t == 0:
            for fc in range(2):
                if 2 * h + fc:
                    own_copies[2 * h + fc].wait_recv()
        else:
            z_copy(t, h, 0).wait_recv()
        for up in range(2):
            @pl.when(z_needed(t, up))
            def _():
                z_copy(t, h, up).start()
        for e in range(1, X):
            x_copy(t, h, e).start()

    def flatten(first, last):
        @pl.loop(first // 2, last // 2)
        def _(pairno):
            for slot in range(2):
                i = pairno * 2 + slot
                load(i, slot).wait()
                rows = pl.ds(pl.multiple_of(i * CHUNK, CHUNK), CHUNK)
                vbuf[rows, :] = stage[slot].reshape(CHUNK, N)

                @pl.when(i + 2 < chunks)
                def _():
                    load(i + 2, slot).start()

    c_copies, y_copies = {}, {}

    def multiply(t):
        s = source(t)
        for e in range(1, X):
            for h in range(Y):
                x_copy(t, h, e).wait_recv()

        @pl.loop(0, N // step_cols)
        def _(n):
            at = pl.ds(pl.multiple_of(n * step_cols, step_cols), step_cols)
            rows = tbuf[s].reshape(X * O * 16, K)
            product = jnp.dot(rows, vbuf[:, at], preferred_element_type=jnp.float32)
            part[t, :, :, :, :, at] = (product * keep_ref[pl.ds(n * step_cols // cols, 1), :]).reshape(X, Y, 2, 16, step_cols)

        c_copies[t] = remote(part.at[t, :, :, 1], core_in.at[t], c_send.at[t], c_recv.at[t], {"own": own_at(0, 1)})
        c_copies[t].start()

    def add_core(t):
        c_copies[t].wait_recv()
        for fy in list(range(1, Y)) + [0]:
            for e in range(X):
                part[t, e, fy, 0] = part[t, e, fy, 0] + core_in[t, e, fy]
            if fy:
                y_copies[t, fy] = remote(
                    part.at[t, :, fy, 0], side_in.at[t, fy], y_send.at[t, fy], y_recv.at[t, fy],
                    {"own": own_at(-fy, 0)},
                )
                y_copies[t, fy].start()

    def o_copy(t, e):
        return remote(
            done.at[t, e], out_ref.at[pair], o_send.at[t, e], o_recv.at[z, e], {"pairs": source(t) * X + x_at(-e)}
        )

    def add_side(t):
        for fy in range(1, Y):
            y_copies[t, fy].wait_recv()
        for e in range(X):
            total = part[t, e, 0, 0]
            for fy in range(1, Y):
                total = total + side_in[t, fy, e]
            rounded = total.astype(jnp.bfloat16)
            if t == 0 and e == 0:
                out_ref[pair] = rounded
            else:
                done[t, e] = rounded
                o_copy(t, e).start()

    early = [(0, h) for h in range(Y)] + [(t, h) for h in range(Y) for t in range(1, min(3, Z))]
    cuts = [chunks * k // (len(early) - 1) // 2 * 2 for k in range(len(early))]
    for k, (t, h) in enumerate(early):
        if k:
            flatten(cuts[k - 1], cuts[k])
        arrive(t, h)
    for t in range(Z):
        if t == 0 and Z > 3:
            arrive(3, 0)
        multiply(t)
        if t + 3 < Z:
            for h in range(1, Y):
                arrive(t + 3, h)
            if t + 4 < Z:
                arrive(t + 4, 0)
        if t >= 1:
            add_core(t - 1)
        if t >= 2:
            add_side(t - 2)
    add_core(Z - 1)
    add_side(Z - 2)
    add_side(Z - 1)
    for t in range(Z):
        for e in range(X):
            if t or e:
                s = source(t)
                remote(
                    done.at[t, e], out_ref.at[s * X + x_at(e)], o_send.at[t, e], o_recv.at[s, e], {"pairs": s * X + x_at(e)}
                ).wait_recv()
                o_copy(t, e).wait_send()
    for t in range(Z):
        for h in range(Y):
            for up in range(2):
                @pl.when(z_needed(t, up))
                def _():
                    z_copy(t, h, up).wait_send()
            for e in range(1, X):
                x_copy(t, h, e).wait_send()
    for group in (own_copies, c_copies, y_copies):
        for copy in group.values():
            copy.wait_send()


def local(amplitudes, integrals, owner, amp_mask, int_mask, out_mask):
    own_count = lax.axis_size("own")
    pairs_count = lax.axis_size("pairs")
    slab = integrals[0]
    piece_rows, tile_count, col_count = slab.shape
    pair_rows, panel_count, tile_pair = amplitudes.shape
    width = tile_count * col_count
    X = math.isqrt(pairs_count // 2)
    Z = pairs_count // X
    Y = own_count // 2
    place = lax.axis_index("own")
    split = tile_pair // piece_rows
    step_cols = min(256, col_count)
    piece_mask = jnp.repeat(int_mask, split, axis=0)
    mine = (owner == place)[:, None]
    chosen = jnp.sum(jnp.where(mine, piece_mask, 0), axis=0) * out_mask
    keep = jnp.broadcast_to(chosen.astype(jnp.float32)[:, None], (tile_count, step_cols))
    pieces = amplitudes.reshape(pair_rows, own_count, piece_rows)
    slots = jnp.arange(own_count, dtype=jnp.int32)
    used = jnp.repeat(amp_mask, split, axis=1)[None, :, :] * (owner[None, None, :] == slots[:, None, None])
    ordered = jnp.sum(
        jnp.where(used[..., None] != 0, pieces[None].astype(jnp.float32), 0), axis=2
    ).astype(jnp.bfloat16)
    sizes = (Z, X, Y, piece_rows, width, col_count, step_cols)
    dma = lambda *shape: pltpu.SemaphoreType.DMA(shape)
    vmem = pl.BlockSpec(memory_space=pltpu.VMEM)
    moved = pl.pallas_call(
        functools.partial(kernel, sizes),
        out_shape=jax.ShapeDtypeStruct((pairs_count, pair_rows, width), jnp.bfloat16),
        in_specs=[vmem, pl.BlockSpec(memory_space=pl.ANY), vmem],
        out_specs=vmem,
        scratch_shapes=[
            pltpu.VMEM((Z, X, Y, 2, pair_rows, piece_rows), jnp.bfloat16),
            pltpu.VMEM((piece_rows, width), jnp.bfloat16),
            pltpu.VMEM((2, CHUNK, tile_count, col_count), jnp.bfloat16),
            pltpu.VMEM((Z, X, Y, 2, pair_rows, width), jnp.float32),
            pltpu.VMEM((Z, X, Y, pair_rows, width), jnp.float32),
            pltpu.VMEM((Z, Y, X, pair_rows, width), jnp.float32),
            pltpu.VMEM((Z, X, pair_rows, width), jnp.bfloat16),
            dma(2), dma(own_count), dma(own_count), dma(Z, Y, 2), dma(Z, Y), dma(Z, Y, X), dma(Z, Y, X),
            dma(Z), dma(Z), dma(Z, Y), dma(Z, Y), dma(Z, X), dma(Z, X),
        ],
        compiler_params=pltpu.CompilerParams(
            collective_id=0, has_side_effects=True, vmem_limit_bytes=60 * 1024 * 1024
        ),
        cost_estimate=pl.CostEstimate(
            flops=2 * pairs_count * own_count * pair_rows * piece_rows * width,
            bytes_accessed=2 * piece_rows * width, transcendentals=0,
        ),
    )(ordered, slab, keep)
    shaped = moved.reshape(pairs_count, pair_rows, tile_count, col_count)
    return jnp.transpose(shaped, (1, 2, 0, 3)).reshape(pair_rows, tile_count, pairs_count * col_count)


def solution(mesh):
    return jax.shard_map(
        local,
        mesh=mesh,
        in_specs=(
            P(("pairs", "own"), None, None),
            P("own", None, None, "pairs"),
            P(),
            P(("pairs", "own"), None),
            P(),
            P(),
        ),
        out_specs=P(("pairs", "own"), None, None),
        check_vma=False,
    )
```

```python
import functools
import math

import jax
import jax.numpy as jnp
from jax import lax
from jax.experimental import pallas as pl
from jax.experimental.pallas import tpu as pltpu
from jax.sharding import PartitionSpec as P

MESH = pl.DeviceIdType.MESH
CHUNK = 256


def kernel(sizes, t_ref, v_ref, owner_ref, int_ref, mask_ref, out_ref, tbuf, vbuf, stage, part, core_in, side_in, done,
           v_sem, own_send, own_recv, z_send, z_recv, x_send, x_recv, c_send, c_recv, y_send, y_recv, o_send, o_recv):
    Z, X, Y, K, N, cols, step_cols = sizes
    O, PAIRS = 2 * Y, Z * X
    pair, own = lax.axis_index("pairs"), lax.axis_index("own")
    z, x = pair // X, pair % X
    y, c = own // 2, own % 2
    near = jnp.minimum(z, Z - 1 - z)
    longer = jnp.where(2 * z < Z - 1, 1, -1)

    def own_at(fy, fc):
        return ((y + Y + fy) % Y) * 2 + (c + 2 + fc) % 2

    def x_at(e):
        return (x + X + e) % X

    def source(t):
        if t == 0:
            return z
        both = z + (t + 1) // 2 * (1 if t % 2 else -1)
        return jnp.where(t <= 2 * near, both, z + longer * (t - near))

    def remote(src, dst, send, recv, device):
        return pltpu.make_async_remote_copy(
            src_ref=src, dst_ref=dst, send_sem=send, recv_sem=recv, device_id=device, device_id_type=MESH
        )

    barrier = pltpu.get_barrier_semaphore()
    for f in range(1, O):
        pl.semaphore_signal(barrier, inc=1, device_id={"own": (own + f) % O}, device_id_type=MESH)
    for g in range(1, PAIRS):
        pl.semaphore_signal(barrier, inc=1, device_id={"pairs": (pair + g) % PAIRS}, device_id_type=MESH)

    chunks = K // CHUNK

    def load(i, slot):
        rows = pl.ds(pl.multiple_of(i * CHUNK, CHUNK), CHUNK)
        return pltpu.make_async_copy(v_ref.at[rows], stage.at[slot], v_sem.at[slot])

    load(0, 0).start()
    load(1, 1).start()
    pl.semaphore_wait(barrier, O - 1 + PAIRS - 1)

    own_copies = {}
    for f in range(1, O):
        fy, fc = f // 2, f % 2
        to = own_at(fy, fc)
        own_copies[f] = remote(t_ref.at[to], tbuf.at[z, 0, fy, fc], own_send.at[f], own_recv.at[f], {"own": to})
        own_copies[f].start()
    tbuf[z, 0, 0, 0] = t_ref[own]

    def z_copy(t, h, up):
        s = source(t)
        to = jnp.where(up == 1, jnp.minimum(z + 1, Z - 1), jnp.maximum(z - 1, 0))
        block = tbuf.at[s, 0, h]
        return remote(block, block, z_send.at[t, h, up], z_recv.at[s, h], {"pairs": to * X + x})

    def z_needed(t, up):
        s = source(t)
        if up:
            return jnp.logical_and(s <= z, z + 1 < Z)
        return jnp.logical_and(s >= z, z >= 1)

    def x_copy(t, h, e):
        s = source(t)
        return remote(
            tbuf.at[s, 0, h], tbuf.at[s, e, h], x_send.at[t, h, e], x_recv.at[t, h, e], {"pairs": z * X + x_at(e)}
        )

    def arrive(t, h):
        if t == 0:
            for fc in range(2):
                if 2 * h + fc:
                    own_copies[2 * h + fc].wait_recv()
        else:
            z_copy(t, h, 0).wait_recv()
        for up in range(2):
            @pl.when(z_needed(t, up))
            def _():
                z_copy(t, h, up).start()
        for e in range(1, X):
            x_copy(t, h, e).start()

    def flatten(first, last):
        @pl.loop(first // 2, last // 2)
        def _(pairno):
            for slot in range(2):
                i = pairno * 2 + slot
                load(i, slot).wait()
                rows = pl.ds(pl.multiple_of(i * CHUNK, CHUNK), CHUNK)
                vbuf[rows, :] = stage[slot].reshape(CHUNK, N)

                @pl.when(i + 2 < chunks)
                def _():
                    load(i + 2, slot).start()

    def kept(tile):
        entry = 0
        for piece in range(O):
            entry = entry + jnp.where(owner_ref[piece] == own, int_ref[piece * int_ref.shape[0] // O, tile], 0)
        return (entry * mask_ref[tile]).astype(jnp.float32)

    c_copies, y_copies = {}, {}

    def multiply(t):
        s = source(t)
        for e in range(1, X):
            for h in range(Y):
                x_copy(t, h, e).wait_recv()

        @pl.loop(0, N // step_cols)
        def _(n):
            at = pl.ds(pl.multiple_of(n * step_cols, step_cols), step_cols)
            rows = tbuf[s].reshape(X * O * 16, K)
            product = jnp.dot(rows, vbuf[:, at], preferred_element_type=jnp.float32)
            part[t, :, :, :, :, at] = (product * kept(n * step_cols // cols)).reshape(X, Y, 2, 16, step_cols)

        c_copies[t] = remote(part.at[t, :, :, 1], core_in.at[t], c_send.at[t], c_recv.at[t], {"own": own_at(0, 1)})
        c_copies[t].start()

    def add_core(t):
        c_copies[t].wait_recv()
        for fy in list(range(1, Y)) + [0]:
            for e in range(X):
                part[t, e, fy, 0] = part[t, e, fy, 0] + core_in[t, e, fy]
            if fy:
                y_copies[t, fy] = remote(
                    part.at[t, :, fy, 0], side_in.at[t, fy], y_send.at[t, fy], y_recv.at[t, fy],
                    {"own": own_at(-fy, 0)},
                )
                y_copies[t, fy].start()

    def o_copy(t, e):
        return remote(
            done.at[t, e], out_ref.at[pair], o_send.at[t, e], o_recv.at[z, e], {"pairs": source(t) * X + x_at(-e)}
        )

    def add_side(t):
        for fy in range(1, Y):
            y_copies[t, fy].wait_recv()
        for e in range(X):
            total = part[t, e, 0, 0]
            for fy in range(1, Y):
                total = total + side_in[t, fy, e]
            rounded = total.astype(jnp.bfloat16)
            if t == 0 and e == 0:
                out_ref[pair] = rounded
            else:
                done[t, e] = rounded
                o_copy(t, e).start()

    early = [(0, h) for h in range(Y)] + [(t, h) for h in range(Y) for t in range(1, min(3, Z))]
    cuts = [chunks * k // (len(early) - 1) // 2 * 2 for k in range(len(early))]
    for k, (t, h) in enumerate(early):
        if k:
            flatten(cuts[k - 1], cuts[k])
        arrive(t, h)
    for t in range(Z):
        if t == 0 and Z > 3:
            arrive(3, 0)
        multiply(t)
        if t + 3 < Z:
            for h in range(1, Y):
                arrive(t + 3, h)
            if t + 4 < Z:
                arrive(t + 4, 0)
        if t >= 1:
            add_core(t - 1)
        if t >= 2:
            add_side(t - 2)
    add_core(Z - 1)
    add_side(Z - 2)
    add_side(Z - 1)
    for t in range(Z):
        for e in range(X):
            if t or e:
                s = source(t)
                remote(
                    done.at[t, e], out_ref.at[s * X + x_at(e)], o_send.at[t, e], o_recv.at[s, e], {"pairs": s * X + x_at(e)}
                ).wait_recv()
                o_copy(t, e).wait_send()
    for t in range(Z):
        for h in range(Y):
            for up in range(2):
                @pl.when(z_needed(t, up))
                def _():
                    z_copy(t, h, up).wait_send()
            for e in range(1, X):
                x_copy(t, h, e).wait_send()
    for group in (own_copies, c_copies, y_copies):
        for copy in group.values():
            copy.wait_send()


def local(amplitudes, integrals, owner, amp_mask, int_mask, out_mask):
    own_count = lax.axis_size("own")
    pairs_count = lax.axis_size("pairs")
    slab = integrals[0]
    piece_rows, tile_count, col_count = slab.shape
    pair_rows, panel_count, tile_pair = amplitudes.shape
    width = tile_count * col_count
    X = math.isqrt(pairs_count // 2)
    Z = pairs_count // X
    Y = own_count // 2
    split = tile_pair // piece_rows
    step_cols = min(256, col_count)
    pieces = amplitudes.reshape(pair_rows, own_count, piece_rows)
    slots = jnp.arange(own_count, dtype=jnp.int32)
    used = jnp.repeat(amp_mask, split, axis=1)[None, :, :] * (owner[None, None, :] == slots[:, None, None])
    ordered = jnp.sum(
        jnp.where(used[..., None] != 0, pieces[None].astype(jnp.float32), 0), axis=2
    ).astype(jnp.bfloat16)
    sizes = (Z, X, Y, piece_rows, width, col_count, step_cols)
    dma = lambda *shape: pltpu.SemaphoreType.DMA(shape)
    vmem = pl.BlockSpec(memory_space=pltpu.VMEM)
    moved = pl.pallas_call(
        functools.partial(kernel, sizes),
        out_shape=jax.ShapeDtypeStruct((pairs_count, pair_rows, width), jnp.bfloat16),
        in_specs=[vmem, pl.BlockSpec(memory_space=pl.ANY)] + [pl.BlockSpec(memory_space=pltpu.SMEM)] * 3,
        out_specs=vmem,
        scratch_shapes=[
            pltpu.VMEM((Z, X, Y, 2, pair_rows, piece_rows), jnp.bfloat16),
            pltpu.VMEM((piece_rows, width), jnp.bfloat16),
            pltpu.VMEM((2, CHUNK, tile_count, col_count), jnp.bfloat16),
            pltpu.VMEM((Z, X, Y, 2, pair_rows, width), jnp.float32),
            pltpu.VMEM((Z, X, Y, pair_rows, width), jnp.float32),
            pltpu.VMEM((Z, Y, X, pair_rows, width), jnp.float32),
            pltpu.VMEM((Z, X, pair_rows, width), jnp.bfloat16),
            dma(2), dma(own_count), dma(own_count), dma(Z, Y, 2), dma(Z, Y), dma(Z, Y, X), dma(Z, Y, X),
            dma(Z), dma(Z), dma(Z, Y), dma(Z, Y), dma(Z, X), dma(Z, X),
        ],
        compiler_params=pltpu.CompilerParams(
            collective_id=0, has_side_effects=True, vmem_limit_bytes=60 * 1024 * 1024
        ),
        cost_estimate=pl.CostEstimate(
            flops=2 * pairs_count * own_count * pair_rows * piece_rows * width,
            bytes_accessed=2 * piece_rows * width, transcendentals=0,
        ),
    )(ordered, slab, owner, int_mask, out_mask)
    shaped = moved.reshape(pairs_count, pair_rows, tile_count, col_count)
    return jnp.transpose(shaped, (1, 2, 0, 3)).reshape(pair_rows, tile_count, pairs_count * col_count)


def solution(mesh):
    return jax.shard_map(
        local,
        mesh=mesh,
        in_specs=(
            P(("pairs", "own"), None, None),
            P("own", None, None, "pairs"),
            P(),
            P(("pairs", "own"), None),
            P(),
            P(),
        ),
        out_specs=P(("pairs", "own"), None, None),
        check_vma=False,
    )
```

```python
import functools
import math

import jax
import jax.numpy as jnp
from jax import lax
from jax.experimental import pallas as pl
from jax.experimental.pallas import tpu as pltpu
from jax.sharding import PartitionSpec as P

MESH = pl.DeviceIdType.MESH
CHUNK = 256


def kernel(sizes, t_ref, v_ref, owner_ref, int_ref, mask_ref, out_ref, tbuf, vbuf, stage, part, core_in, side_in, done,
           v_sem, own_send, own_recv, z_send, z_recv, x_send, x_recv, c_send, c_recv, y_send, y_recv, o_send, o_recv):
    Z, X, Y, K, N, cols, step_cols = sizes
    O, PAIRS = 2 * Y, Z * X
    pair, own = lax.axis_index("pairs"), lax.axis_index("own")
    z, x = pair // X, pair % X
    y, c = own // 2, own % 2
    near = jnp.minimum(z, Z - 1 - z)
    longer = jnp.where(2 * z < Z - 1, 1, -1)

    def own_at(fy, fc):
        return ((y + Y + fy) % Y) * 2 + (c + 2 + fc) % 2

    def x_at(e):
        return (x + X + e) % X

    def source(t):
        if t == 0:
            return z
        both = z + (t + 1) // 2 * (1 if t % 2 else -1)
        return jnp.where(t <= 2 * near, both, z + longer * (t - near))

    def remote(src, dst, send, recv, device):
        return pltpu.make_async_remote_copy(
            src_ref=src, dst_ref=dst, send_sem=send, recv_sem=recv, device_id=device, device_id_type=MESH
        )

    barrier = pltpu.get_barrier_semaphore()
    for f in range(1, O):
        pl.semaphore_signal(barrier, inc=1, device_id={"own": (own + f) % O}, device_id_type=MESH)
    for g in range(1, PAIRS):
        pl.semaphore_signal(barrier, inc=1, device_id={"pairs": (pair + g) % PAIRS}, device_id_type=MESH)

    chunks = K // CHUNK

    def load(i, slot):
        rows = pl.ds(pl.multiple_of(i * CHUNK, CHUNK), CHUNK)
        return pltpu.make_async_copy(v_ref.at[rows], stage.at[slot], v_sem.at[slot])

    load(0, 0).start()
    load(1, 1).start()
    pl.semaphore_wait(barrier, O - 1 + PAIRS - 1)

    own_copies = {}
    for f in range(1, O):
        fy, fc = f // 2, f % 2
        to = own_at(fy, fc)
        own_copies[f] = remote(t_ref.at[to], tbuf.at[z, 0, fy, fc], own_send.at[f], own_recv.at[f], {"own": to})
        own_copies[f].start()
    tbuf[z, 0, 0, 0] = t_ref[own]

    def z_copy(t, h, up):
        s = source(t)
        to = jnp.where(up == 1, jnp.minimum(z + 1, Z - 1), jnp.maximum(z - 1, 0))
        block = tbuf.at[s, 0, h]
        return remote(block, block, z_send.at[t, h, up], z_recv.at[s, h], {"pairs": to * X + x})

    def z_needed(t, up):
        s = source(t)
        if up:
            return jnp.logical_and(s <= z, z + 1 < Z)
        return jnp.logical_and(s >= z, z >= 1)

    def x_copy(t, h, e):
        s = source(t)
        return remote(
            tbuf.at[s, 0, h], tbuf.at[s, e, h], x_send.at[t, h, e], x_recv.at[t, h, e], {"pairs": z * X + x_at(e)}
        )

    def arrive(t, h):
        if t == 0:
            for fc in range(2):
                if 2 * h + fc:
                    own_copies[2 * h + fc].wait_recv()
        else:
            z_copy(t, h, 0).wait_recv()
        for up in range(2):
            @pl.when(z_needed(t, up))
            def _():
                z_copy(t, h, up).start()
        for e in range(1, X):
            x_copy(t, h, e).start()

    def flatten(first, last):
        @pl.loop(first // 2, last // 2)
        def _(pairno):
            for slot in range(2):
                i = pairno * 2 + slot
                load(i, slot).wait()
                rows = pl.ds(pl.multiple_of(i * CHUNK, CHUNK), CHUNK)
                vbuf[rows, :] = stage[slot].reshape(CHUNK, N)

                @pl.when(i + 2 < chunks)
                def _():
                    load(i + 2, slot).start()

    def kept(tile):
        entry = 0
        for piece in range(O):
            entry = entry + jnp.where(owner_ref[piece] == own, int_ref[piece * int_ref.shape[0] // O, tile], 0)
        return (entry * mask_ref[tile]).astype(jnp.float32)

    c_copies, y_copies = {}, {}

    def multiply(t):
        s = source(t)
        for e in range(1, X):
            for h in range(Y):
                x_copy(t, h, e).wait_recv()

        @pl.loop(0, N // step_cols)
        def _(n):
            at = pl.ds(pl.multiple_of(n * step_cols, step_cols), step_cols)
            rows = tbuf[s].reshape(X * O * 16, K)
            product = jnp.dot(rows, vbuf[:, at], preferred_element_type=jnp.float32)
            part[t, :, :, :, :, at] = (product * kept(n * step_cols // cols)).reshape(X, Y, 2, 16, step_cols)

        c_copies[t] = remote(part.at[t, :, :, 1], core_in.at[t], c_send.at[t], c_recv.at[t], {"own": own_at(0, 1)})
        c_copies[t].start()

    def add_core(t):
        c_copies[t].wait_recv()
        for fy in list(range(1, Y)) + [0]:
            for e in range(X):
                part[t, e, fy, 0] = part[t, e, fy, 0] + core_in[t, e, fy]
            if fy:
                y_copies[t, fy] = remote(
                    part.at[t, :, fy, 0], side_in.at[t, fy], y_send.at[t, fy], y_recv.at[t, fy],
                    {"own": own_at(-fy, 0)},
                )
                y_copies[t, fy].start()

    def o_copy(t, e):
        return remote(
            done.at[t, e], out_ref.at[pair], o_send.at[t, e], o_recv.at[z, e], {"pairs": source(t) * X + x_at(-e)}
        )

    def add_side(t):
        for fy in range(1, Y):
            y_copies[t, fy].wait_recv()
        for e in range(X):
            total = part[t, e, 0, 0]
            for fy in range(1, Y):
                total = total + side_in[t, fy, e]
            rounded = total.astype(jnp.bfloat16)
            if t == 0 and e == 0:
                out_ref[pair] = rounded
            else:
                done[t, e] = rounded
                o_copy(t, e).start()

    early = [(0, h) for h in range(Y)] + [(t, h) for h in range(Y) for t in range(1, min(3, Z))]
    cuts = [chunks * k // (len(early) - 1) // 2 * 2 for k in range(len(early))]
    for k, (t, h) in enumerate(early):
        if k:
            flatten(cuts[k - 1], cuts[k])
        arrive(t, h)
    for t in range(Z):
        if t + 3 < Z:
            for h in range(Y):
                arrive(t + 3, h)
        multiply(t)
        if t >= 1:
            add_core(t - 1)
        if t >= 2:
            add_side(t - 2)
    add_core(Z - 1)
    add_side(Z - 2)
    add_side(Z - 1)
    for t in range(Z):
        for e in range(X):
            if t or e:
                s = source(t)
                remote(
                    done.at[t, e], out_ref.at[s * X + x_at(e)], o_send.at[t, e], o_recv.at[s, e], {"pairs": s * X + x_at(e)}
                ).wait_recv()
                o_copy(t, e).wait_send()
    for t in range(Z):
        for h in range(Y):
            for up in range(2):
                @pl.when(z_needed(t, up))
                def _():
                    z_copy(t, h, up).wait_send()
            for e in range(1, X):
                x_copy(t, h, e).wait_send()
    for group in (own_copies, c_copies, y_copies):
        for copy in group.values():
            copy.wait_send()


def local(amplitudes, integrals, owner, amp_mask, int_mask, out_mask):
    own_count = lax.axis_size("own")
    pairs_count = lax.axis_size("pairs")
    slab = integrals[0]
    piece_rows, tile_count, col_count = slab.shape
    pair_rows, panel_count, tile_pair = amplitudes.shape
    width = tile_count * col_count
    X = math.isqrt(pairs_count // 2)
    Z = pairs_count // X
    Y = own_count // 2
    split = tile_pair // piece_rows
    step_cols = min(256, col_count)
    pieces = amplitudes.reshape(pair_rows, own_count, piece_rows)
    slots = jnp.arange(own_count, dtype=jnp.int32)
    used = jnp.repeat(amp_mask, split, axis=1)[None, :, :] * (owner[None, None, :] == slots[:, None, None])
    ordered = jnp.sum(
        jnp.where(used[..., None] != 0, pieces[None].astype(jnp.float32), 0), axis=2
    ).astype(jnp.bfloat16)
    sizes = (Z, X, Y, piece_rows, width, col_count, step_cols)
    dma = lambda *shape: pltpu.SemaphoreType.DMA(shape)
    vmem = pl.BlockSpec(memory_space=pltpu.VMEM)
    moved = pl.pallas_call(
        functools.partial(kernel, sizes),
        out_shape=jax.ShapeDtypeStruct((pairs_count, pair_rows, width), jnp.bfloat16),
        in_specs=[vmem, pl.BlockSpec(memory_space=pl.ANY)] + [pl.BlockSpec(memory_space=pltpu.SMEM)] * 3,
        out_specs=vmem,
        scratch_shapes=[
            pltpu.VMEM((Z, X, Y, 2, pair_rows, piece_rows), jnp.bfloat16),
            pltpu.VMEM((piece_rows, width), jnp.bfloat16),
            pltpu.VMEM((2, CHUNK, tile_count, col_count), jnp.bfloat16),
            pltpu.VMEM((Z, X, Y, 2, pair_rows, width), jnp.float32),
            pltpu.VMEM((Z, X, Y, pair_rows, width), jnp.float32),
            pltpu.VMEM((Z, Y, X, pair_rows, width), jnp.float32),
            pltpu.VMEM((Z, X, pair_rows, width), jnp.bfloat16),
            dma(2), dma(own_count), dma(own_count), dma(Z, Y, 2), dma(Z, Y), dma(Z, Y, X), dma(Z, Y, X),
            dma(Z), dma(Z), dma(Z, Y), dma(Z, Y), dma(Z, X), dma(Z, X),
        ],
        compiler_params=pltpu.CompilerParams(
            collective_id=0, has_side_effects=True, vmem_limit_bytes=60 * 1024 * 1024
        ),
        cost_estimate=pl.CostEstimate(
            flops=2 * pairs_count * own_count * pair_rows * piece_rows * width,
            bytes_accessed=2 * piece_rows * width, transcendentals=0,
        ),
    )(ordered, slab, owner, int_mask, out_mask)
    shaped = moved.reshape(pairs_count, pair_rows, tile_count, col_count)
    return jnp.transpose(shaped, (1, 2, 0, 3)).reshape(pair_rows, tile_count, pairs_count * col_count)


def solution(mesh):
    return jax.shard_map(
        local,
        mesh=mesh,
        in_specs=(
            P(("pairs", "own"), None, None),
            P("own", None, None, "pairs"),
            P(),
            P(("pairs", "own"), None),
            P(),
            P(),
        ),
        out_specs=P(("pairs", "own"), None, None),
        check_vma=False,
    )
```
